32 devices in a mesh: groups: 2 (over y), row: 4 (over z), col: 4 (over x, core).
Axes of the slice: x: 2, y: 2, z: 4, core: 2. Of those that a mesh axis runs over, the one named last changes fastest.
Arguments:
- view_a: bfloat16 [4096, 8192], P(('groups', 'col'), 'row'), parts along dimension 0, may hold values from -100 to 100
- view_b: bfloat16 [4096, 8192], P(('groups', 'row'), 'col'), parts along dimension 0, may hold values from -100 to 100
Outputs:
- grad_a: float32 [4096, 8192], P(('groups', 'col'), 'row'), parts along dimension 0
- grad_b: float32 [4096, 8192], P(('groups', 'row'), 'col'), parts along dimension 0
The draws below stay inside these ranges and needn't reach their ends.
There are 2 independent parts, one for each index of `groups`. The reference program is written for one: setup_inputs(seed, part) draws one part's arguments, and reference() takes and returns one part's arrays. A program takes and returns all parts, laid end to end along the dimension named above; each array names one. Nothing has to cross between parts.
All inputs are finite; a program needn't handle non-finite values.
Results may differ from the reference program's by a relative error of at most 0.0069.
Values may be sent and summed in bfloat16 or wider, within the bound.
A program may use at most 192 MiB of HBM per device.

```python
import math
import jax
import jax.numpy as jnp
from jax import lax

D = 8192
IMG = 2048


def common(key):
    key_gauss = jax.random.fold_in(key, 0)
    key_rows = jax.random.fold_in(key, 2)
    gauss_base = jnp.clip(jax.random.normal(key_gauss, (IMG, D), jnp.float32), -6.0, 6.0)
    row_draw = jax.random.uniform(key_rows, (IMG, 1), jnp.float32)
    return (gauss_base, row_draw)


def column_factors(key):
    key_scale, key_shift = jax.random.split(key, 2)
    low = math.log(0.3)
    high = math.log(3.0)
    column_scale = jnp.exp(jax.random.uniform(key_scale, (1, D), jnp.float32, low, high))
    column_shift = jnp.clip(jax.random.normal(key_shift, (1, D), jnp.float32), -6.0, 6.0)
    return (column_scale, column_shift)


def draw_view_a(key, part):
    gauss_base, row_draw = common(key)
    key = jax.random.fold_in(key, 11)
    column_scale, column_shift = column_factors(key)
    row_scale = jnp.exp(row_draw * math.log(10.0)) / 3.0
    values = 0.5 * column_shift + row_scale * column_scale * gauss_base
    return values.astype(jnp.bfloat16)


def draw_view_b(key, part):
    gauss_base, row_draw = common(key)
    key = jax.random.fold_in(key, 23)
    key_noise, key_cols = jax.random.split(key, 2)
    column_scale, column_shift = column_factors(key_cols)
    noise = jnp.clip(jax.random.normal(key_noise, (IMG, D), jnp.float32), -6.0, 6.0)
    row_scale = jnp.exp(row_draw * math.log(10.0)) / 3.0
    mixed = 0.9 * gauss_base + 0.436 * noise
    values = 0.5 * column_shift + row_scale * column_scale * mixed
    return values.astype(jnp.bfloat16)


def setup_inputs(seed: int = 0, part: int = 0) -> dict:
    key_of = jax.random.split(jax.random.key(seed), 3)
    part_keys = jax.random.split(jax.random.fold_in(key_of[2], part), 3)
    return {
        "view_a": draw_view_a(jax.random.fold_in(jax.random.fold_in(key_of[2], part), 71), part),
        "view_b": draw_view_b(jax.random.fold_in(jax.random.fold_in(key_of[2], part), 71), part),
    }


EPSILON = 1e-05
OFF_WEIGHT = 0.0051

def standardize(view):
    values = view.astype(jnp.float32)
    column_mean = lax.optimization_barrier(jnp.mean(values, axis=0))
    centered = values - column_mean
    variance = lax.optimization_barrier(jnp.mean(centered * centered, axis=0))
    scale = lax.rsqrt(variance + EPSILON)
    return (centered * scale, scale)

def view_grad(back, unit, scale):
    mean_back = lax.optimization_barrier(jnp.mean(back, axis=0))
    mean_proj = lax.optimization_barrier(jnp.mean(back * unit, axis=0))
    return scale * (back - mean_back - unit * mean_proj)

def reference(view_a, view_b):
    unit_a, scale_a = standardize(view_a)
    unit_b, scale_b = standardize(view_b)
    norm_a = unit_a.astype(jnp.bfloat16).astype(jnp.float32)
    norm_b = unit_b.astype(jnp.bfloat16).astype(jnp.float32)
    correlation = jnp.dot(norm_a.T, norm_b, preferred_element_type=jnp.float32) / IMG
    index = jnp.arange(D)
    on_diagonal = index[:, None] == index[None, :]
    grad_corr = jnp.where(on_diagonal, 2.0 * (correlation - 1.0), 2.0 * OFF_WEIGHT * correlation)
    grad_corr = grad_corr.astype(jnp.bfloat16).astype(jnp.float32)
    back_a = jnp.dot(norm_b, grad_corr.T, preferred_element_type=jnp.float32)
    back_b = jnp.dot(norm_a, grad_corr, preferred_element_type=jnp.float32)
    return (view_grad(back_a, unit_a, scale_a), view_grad(back_b, unit_b, scale_b))
```

```python
import jax
import jax.numpy as jnp
from jax import lax
from jax.sharding import PartitionSpec as P

EPSILON = 1e-05
OFF_WEIGHT = 0.0051


def standardize(full_view):
    values = full_view.astype(jnp.float32)
    images = values.shape[0]
    column_mean = jnp.sum(values, axis=0) / images
    centered = values - column_mean
    variance = jnp.sum(centered * centered, axis=0) / images
    scale = lax.rsqrt(variance + EPSILON)
    unit_full = centered * scale
    return (unit_full, unit_full.astype(jnp.bfloat16), scale)


def per_device_corr(view_a, view_b):
    rows_a, width_a = view_a.shape
    rows_b, width_b = view_b.shape
    col_count = lax.axis_size("col")
    row_index = lax.axis_index("row")
    col_index = lax.axis_index("col")
    full_a = lax.all_gather(view_a, "col", axis=0, tiled=True)
    full_b = lax.all_gather(view_b, "row", axis=0, tiled=True)
    images = full_a.shape[0]
    unit_a, norm_a, scale_a = standardize(full_a)
    unit_b, norm_b, scale_b = standardize(full_b)
    correlation = (
        lax.dot_general(
            norm_a, norm_b, (((0,), (0,)), ((), ())), preferred_element_type=jnp.float32
        )
        / images
    )
    row_ids = row_index * width_a + jnp.arange(width_a)
    col_ids = col_index * width_b + jnp.arange(width_b)
    on_diagonal = row_ids[:, None] == col_ids[None, :]
    grad_corr = jnp.where(
        on_diagonal, 2.0 * (correlation - 1.0), 2.0 * OFF_WEIGHT * correlation
    ).astype(jnp.bfloat16)
    slab = norm_b
    back_a = lax.psum_scatter(
        lax.dot_general(
            slab, grad_corr, (((1,), (1,)), ((), ())), preferred_element_type=jnp.float32
        ),
        "col",
        scatter_dimension=0,
        tiled=True,
    )
    own_a = lax.dynamic_slice_in_dim(unit_a, col_index * rows_a, rows_a, 0)
    sums_a = jnp.stack([jnp.sum(back_a, axis=0), jnp.sum(back_a * own_a, axis=0)])
    slab = norm_a
    back_b = lax.psum_scatter(
        jnp.dot(slab, grad_corr, preferred_element_type=jnp.float32),
        "row",
        scatter_dimension=0,
        tiled=True,
    )
    own_b = lax.dynamic_slice_in_dim(unit_b, row_index * rows_b, rows_b, 0)
    sums_b = jnp.stack([jnp.sum(back_b, axis=0), jnp.sum(back_b * own_b, axis=0)])
    whole_width = width_b * col_count
    placed_b = lax.dynamic_update_slice(
        jnp.zeros((2, whole_width), jnp.float32), sums_b, (0, col_index * width_b)
    )
    placed_a = lax.dynamic_update_slice(
        jnp.zeros((2, whole_width), jnp.float32), sums_a, (0, row_index * width_a)
    )
    stacked = jnp.concatenate([placed_a, placed_b], axis=0)
    totals = lax.psum(stacked, ("row", "col"))
    total_b = lax.dynamic_slice_in_dim(totals[-2:], col_index * width_b, width_b, 1)
    total_a = lax.dynamic_slice_in_dim(totals[0:2], row_index * width_a, width_a, 1)
    grad_a = scale_a * (back_a - total_a[0] / images - own_a * (total_a[1] / images))
    grad_b = scale_b * (back_b - total_b[0] / images - own_b * (total_b[1] / images))
    return (grad_a, grad_b)


def per_device_gram(view_a, view_b):
    rows, _ = view_a.shape
    side = lax.axis_size("col")
    col_index = lax.axis_index("col")
    swap = [(r * side + c, c * side + r) for r in range(side) for c in range(side)]
    view_b = lax.ppermute(view_b, ("row", "col"), swap)
    full_a = lax.all_gather(view_a, "col", axis=0, tiled=True)
    full_b = lax.all_gather(view_b, "col", axis=0, tiled=True)
    images = full_a.shape[0]
    unit_a, norm_a, scale_a = standardize(full_a)
    unit_b, norm_b, scale_b = standardize(full_b)
    own = lambda x: lax.dynamic_slice_in_dim(x, col_index * rows, rows, 0)

    def gram(norm):
        part = lax.dot_general(
            own(norm), norm, (((1,), (1,)), ((), ())), preferred_element_type=jnp.float32
        )
        return lax.psum(part.astype(jnp.bfloat16), "row")

    gram_a, gram_b = gram(norm_a), gram(norm_b)
    diagonal = (
        jnp.sum(norm_a.astype(jnp.float32) * norm_b.astype(jnp.float32), axis=0) / images
    )
    weight = 2.0 * OFF_WEIGHT
    direct = (2.0 * (diagonal - 1.0)).astype(jnp.bfloat16).astype(jnp.float32)
    direct = direct - weight * diagonal

    def back(gram_other, norm, other):
        mixed = jnp.dot(gram_other, norm, preferred_element_type=jnp.float32)
        return (weight / images) * mixed + direct * own(other).astype(jnp.float32)

    own_a, own_b = own(unit_a), own(unit_b)
    back_b = back(gram_a, norm_b, norm_a)
    back_a = back(gram_b, norm_a, norm_b)
    sums = lax.psum(
        jnp.stack(
            [
                jnp.sum(back_a, axis=0),
                jnp.sum(back_a * own_a, axis=0),
                jnp.sum(back_b, axis=0),
                jnp.sum(back_b * own_b, axis=0),
            ]
        ),
        "col",
    ) / images
    grad_b = scale_b * (back_b - sums[2] - own_b * sums[3])
    grad_b = lax.ppermute(grad_b.astype(jnp.bfloat16), ("row", "col"), swap)
    grad_a = scale_a * (back_a - sums[0] - own_a * sums[1])
    return (grad_a, grad_b.astype(jnp.float32))


def solution(mesh):
    square = mesh.shape["row"] == mesh.shape["col"]
    per_device = per_device_gram if square else per_device_corr
    return jax.shard_map(
        per_device,
        mesh=mesh,
        in_specs=(P(("groups", "col"), "row"), P(("groups", "row"), "col")),
        out_specs=(P(("groups", "col"), "row"), P(("groups", "row"), "col")),
        check_vma=False,
    )
```

```python
import functools

import jax
import jax.numpy as jnp
from jax import lax
from jax.experimental import pallas as pl
from jax.experimental.pallas import tpu as pltpu
from jax.sharding import PartitionSpec as P

EPSILON = 1e-05
OFF_WEIGHT = 0.0051


def standardize(full_view):
    values = full_view.astype(jnp.float32)
    images = values.shape[0]
    column_mean = jnp.sum(values, axis=0) / images
    centered = values - column_mean
    variance = jnp.sum(centered * centered, axis=0) / images
    scale = lax.rsqrt(variance + EPSILON)
    unit_full = centered * scale
    return (unit_full, unit_full.astype(jnp.bfloat16), scale)


def per_device_corr(view_a, view_b):
    rows_a, width_a = view_a.shape
    rows_b, width_b = view_b.shape
    col_count = lax.axis_size("col")
    row_index = lax.axis_index("row")
    col_index = lax.axis_index("col")
    full_a = lax.all_gather(view_a, "col", axis=0, tiled=True)
    full_b = lax.all_gather(view_b, "row", axis=0, tiled=True)
    images = full_a.shape[0]
    unit_a, norm_a, scale_a = standardize(full_a)
    unit_b, norm_b, scale_b = standardize(full_b)
    correlation = (
        lax.dot_general(
            norm_a, norm_b, (((0,), (0,)), ((), ())), preferred_element_type=jnp.float32
        )
        / images
    )
    row_ids = row_index * width_a + jnp.arange(width_a)
    col_ids = col_index * width_b + jnp.arange(width_b)
    on_diagonal = row_ids[:, None] == col_ids[None, :]
    grad_corr = jnp.where(
        on_diagonal, 2.0 * (correlation - 1.0), 2.0 * OFF_WEIGHT * correlation
    ).astype(jnp.bfloat16)
    slab = norm_b
    back_a = lax.psum_scatter(
        lax.dot_general(
            slab, grad_corr, (((1,), (1,)), ((), ())), preferred_element_type=jnp.float32
        ),
        "col",
        scatter_dimension=0,
        tiled=True,
    )
    own_a = lax.dynamic_slice_in_dim(unit_a, col_index * rows_a, rows_a, 0)
    sums_a = jnp.stack([jnp.sum(back_a, axis=0), jnp.sum(back_a * own_a, axis=0)])
    slab = norm_a
    back_b = lax.psum_scatter(
        jnp.dot(slab, grad_corr, preferred_element_type=jnp.float32),
        "row",
        scatter_dimension=0,
        tiled=True,
    )
    own_b = lax.dynamic_slice_in_dim(unit_b, row_index * rows_b, rows_b, 0)
    sums_b = jnp.stack([jnp.sum(back_b, axis=0), jnp.sum(back_b * own_b, axis=0)])
    whole_width = width_b * col_count
    placed_b = lax.dynamic_update_slice(
        jnp.zeros((2, whole_width), jnp.float32), sums_b, (0, col_index * width_b)
    )
    placed_a = lax.dynamic_update_slice(
        jnp.zeros((2, whole_width), jnp.float32), sums_a, (0, row_index * width_a)
    )
    stacked = jnp.concatenate([placed_a, placed_b], axis=0)
    totals = lax.psum(stacked, ("row", "col"))
    total_b = lax.dynamic_slice_in_dim(totals[-2:], col_index * width_b, width_b, 1)
    total_a = lax.dynamic_slice_in_dim(totals[0:2], row_index * width_a, width_a, 1)
    grad_a = scale_a * (back_a - total_a[0] / images - own_a * (total_a[1] / images))
    grad_b = scale_b * (back_b - total_b[0] / images - own_b * (total_b[1] / images))
    return (grad_a, grad_b)


MESH = pl.DeviceIdType.MESH
SIDE = 4
TILE = 256


def gram_kernel(
    images,
    na,
    nb,
    xa,
    xb,
    stats,
    ga,
    gb,
    part,
    landed,
    gram,
    next_row,
    cross,
    band,
    direct,
    sums,
    sums_in,
    grad_send,
    half_in,
    relay,
    final,
    rs_send,
    rs_recv,
    ag_send,
    ag_recv,
    plane_send,
    plane_recv,
    sum_send,
    sum_recv,
    out_send,
    out_recv,
    local_sem,
):
    g = lax.axis_index("groups")
    r = lax.axis_index("row")
    c = lax.axis_index("col")
    rows, width = xa.shape
    half = rows // 2
    chunk = part.shape[1] // SIDE
    x = c // 2
    lo = c % 2
    flip = (c + 2) % SIDE
    meet = 2 * x + r % 2
    weight = 2.0 * OFF_WEIGHT
    norms, raws, backs = (na, nb), (xa, xb), (ga, gb)

    def near(d):
        return (g, r, (c + d) % SIDE)

    def far(d):
        return (g, (r + d) % SIDE, c)

    def copy(src, dst, send, recv, to):
        return pltpu.make_async_remote_copy(
            src_ref=src,
            dst_ref=dst,
            send_sem=send,
            recv_sem=recv,
            device_id=to,
            device_id_type=MESH,
        )

    barrier = pltpu.get_barrier_semaphore()
    for d in range(1, SIDE):
        pl.semaphore_signal(barrier, inc=1, device_id=near(d), device_id_type=MESH)
        pl.semaphore_signal(barrier, inc=1, device_id=far(d), device_id_type=MESH)
    odd = (r + c) % 2 == 1

    @pl.when(odd)
    def _():
        for plane in (c, flip):
            pl.semaphore_signal(
                barrier, inc=1, device_id=(g, plane, meet), device_id_type=MESH
            )
        pl.semaphore_wait(barrier, 2 * SIDE)

    @pl.when(jnp.logical_not(odd))
    def _():
        pl.semaphore_wait(barrier, 2 * (SIDE - 1))

    def chunk_at(owner):
        return pl.ds(pl.multiple_of(owner * chunk, 16), chunk)

    def make_part(v):
        norm = norms[v]

        def body(i, carry):
            left = jnp.where(i < 4, c * rows + (i % 2) * half, lo * rows + x * half)
            right = jnp.where(i < 2, c, jnp.where(i < 4, (c + 1) % SIDE, lo + 2)) * rows
            a = norm[pl.ds(pl.multiple_of(left, half), half), :]
            b = norm[pl.ds(pl.multiple_of(right, rows), rows), :]
            t = lax.dot_general(
                a, b, (((1,), (1,)), ((), ())), preferred_element_type=jnp.float32
            )
            part[v, pl.ds(pl.multiple_of(i * half, half), half), :] = t.astype(jnp.bfloat16)
            return carry

        lax.fori_loop(0, 5, body, 0)

    def rs_copy(v, d):
        owner = (r + d) % SIDE
        return copy(
            part.at[v, chunk_at(owner), :],
            landed.at[v, d - 1],
            rs_send.at[v, d - 1],
            rs_recv.at[v, d - 1],
            far(d),
        )

    def ag_copy(v, d):
        return copy(
            gram.at[v, chunk_at(r), :],
            gram.at[v, chunk_at(r), :],
            ag_send.at[v, d - 1],
            ag_recv.at[v, d - 1],
            far(d),
        )

    def ag_arrival(v, d):
        owner = (r + SIDE - d) % SIDE
        return copy(
            gram.at[v, chunk_at(owner), :],
            gram.at[v, chunk_at(owner), :],
            ag_send.at[v, d - 1],
            ag_recv.at[v, d - 1],
            far(d),
        )

    def reduce(v):
        for d in range(1, SIDE):
            rs_copy(v, d).wait_recv()
        total = part[v, chunk_at(r), :].astype(jnp.float32)
        for d in range(1, SIDE):
            total = total + landed[v, d - 1].astype(jnp.float32)
        gram[v, chunk_at(r), :] = total.astype(jnp.bfloat16)
        for d in range(1, SIDE):
            ag_copy(v, d).start()

    def plane_copies(v):
        return (
            copy(
                gram.at[v, pl.ds(rows, rows), :],
                next_row.at[v],
                plane_send.at[v, 0],
                plane_recv.at[v, 0],
                near(1),
            ),
            copy(
                gram.at[v, pl.ds(2 * rows, half), :],
                cross.at[v],
                plane_send.at[v, 1],
                plane_recv.at[v, 1],
                near(2),
            ),
        )

    def share(v):
        for d in range(1, SIDE):
            ag_arrival(v, d).wait_recv()
        for one in plane_copies(v):
            one.start()

    def turned(block):
        return block.astype(jnp.float32).T.astype(jnp.bfloat16)

    def make_band(v):
        for one in plane_copies(v):
            one.wait_recv()
        band[c] = gram[v, pl.ds(0, rows), :]
        band[(c + 1) % SIDE] = gram[v, pl.ds(rows, rows), :]
        band[(c + 3) % SIDE] = turned(next_row[v])

        @pl.when(x == 0)
        def _():
            band[flip, pl.ds(0, half), :] = gram[v, pl.ds(2 * rows, half), :]
            band[flip, pl.ds(half, half), :] = cross[v]

        @pl.when(x == 1)
        def _():
            band[flip, :, pl.ds(0, half)] = turned(cross[v])
            band[flip, :, pl.ds(half, half)] = turned(gram[v, pl.ds(2 * rows, half), :])

    own = pl.ds(pl.multiple_of(c * rows, rows), rows)

    def unit_of(w, columns):
        mean = stats[pl.ds(2 * w, 1), columns]
        scale = stats[pl.ds(2 * w + 1, 1), columns]
        return (raws[w][:, columns].astype(jnp.float32) - mean) * scale, scale

    def sum_copy(w, d):
        return copy(
            sums.at[w],
            sums_in.at[w, d - 1],
            sum_send.at[w, d - 1],
            sum_recv.at[w, d - 1],
            near(d),
        )

    def make_back(w):
        norm, other, back_ref = norms[w], norms[1 - w], backs[w]

        def body(j, carry):
            columns = pl.ds(pl.multiple_of(j * TILE, TILE), TILE)
            mixed = jnp.zeros((rows, TILE), jnp.float32)
            for block in range(SIDE):
                mixed = mixed + jnp.dot(
                    band[block],
                    norm[pl.ds(block * rows, rows), columns],
                    preferred_element_type=jnp.float32,
                )
            term = direct[:, columns] * other[own, columns].astype(jnp.float32)
            back = (weight / images) * mixed + term
            unit, _ = unit_of(w, columns)
            back_ref[:, columns] = back
            sums[w, pl.ds(0, 1), columns] = jnp.sum(back, axis=0, keepdims=True)
            sums[w, pl.ds(1, 1), columns] = jnp.sum(back * unit, axis=0, keepdims=True)
            return carry

        lax.fori_loop(0, width // TILE, body, 0)
        for d in range(1, SIDE):
            sum_copy(w, d).start()

    def make_grad(w, target):
        for d in range(1, SIDE):
            sum_copy(w, d).wait_recv()

        def body(j, carry):
            columns = pl.ds(pl.multiple_of(j * TILE, TILE), TILE)
            total = sums[w, pl.ds(0, 2), columns]
            for d in range(1, SIDE):
                total = total + sums_in[w, d - 1, pl.ds(0, 2), columns]
            total = total / images
            unit, scale = unit_of(w, columns)
            grad = scale * (backs[w][:, columns] - total[0:1] - unit * total[1:2])
            target[:, columns] = grad.astype(target.dtype)
            return carry

        lax.fori_loop(0, width // TILE, body, 0)

    def make_direct():
        def body(i, acc):
            lines = pl.ds(pl.multiple_of(i * 16, 16), 16)
            prod = na[lines, :].astype(jnp.float32) * nb[lines, :].astype(jnp.float32)
            return acc + prod[0:8] + prod[8:16]

        acc = lax.fori_loop(0, images // 16, body, jnp.zeros((8, width), jnp.float32))
        diagonal = jnp.sum(acc, axis=0, keepdims=True) / images
        rounded = (2.0 * (diagonal - 1.0)).astype(jnp.bfloat16).astype(jnp.float32)
        direct[...] = rounded - weight * diagonal

    sums[...] = jnp.zeros_like(sums)
    for v in range(2):
        make_part(v)
        for d in range(1, SIDE):
            rs_copy(v, d).start()
    make_direct()
    reduce(0)
    reduce(1)
    share(0)
    make_band(0)
    make_back(1)
    make_grad(1, grad_send)

    mine = pl.ds(pl.multiple_of(x * half, half), half)
    theirs = pl.ds(pl.multiple_of((1 - x) * half, half), half)
    swap = copy(
        grad_send.at[theirs, :], half_in, out_send.at[0], out_recv.at[0], near(2)
    )
    swap.start()
    straight = r // 2 == x

    def hop(src, plane, send):
        @pl.when(straight)
        def _():
            copy(
                src, final.at[mine, :], out_send.at[send], out_recv.at[1], (g, plane, meet)
            ).start()

        @pl.when(jnp.logical_not(straight))
        def _():
            copy(src, relay, out_send.at[send], out_recv.at[2], (g, plane, meet)).start()

    @pl.when(c != r)
    def _():
        hop(grad_send.at[mine, :], c, 1)

    @pl.when(c == r)
    def _():
        stay = pltpu.make_async_copy(grad_send.at[mine, :], final.at[mine, :], local_sem)
        stay.start()
        stay.wait()

    swap.wait_recv()

    @pl.when(flip != r)
    def _():
        hop(half_in, flip, 2)

    @pl.when(flip == r)
    def _():
        stay = pltpu.make_async_copy(half_in, relay, local_sem)
        stay.start()
        stay.wait()

    share(1)
    make_band(1)
    make_back(0)
    make_grad(0, ga)

    forward = copy(relay, final.at[mine, :], out_send.at[3], out_recv.at[3], near(2))

    @pl.when(flip != r)
    def _():
        copy(half_in, relay, out_send.at[2], out_recv.at[2], near(2)).wait_recv()

    forward.start()

    @pl.when(c != r)
    def _():
        copy(
            half_in, final.at[mine, :], out_send.at[1], out_recv.at[1], near(2)
        ).wait_recv()

    copy(relay, final.at[theirs, :], out_send.at[3], out_recv.at[3], near(2)).wait_recv()

    def widen(i, carry):
        lines = pl.ds(pl.multiple_of(i * 16, 16), 16)
        gb[lines, :] = final[lines, :].astype(jnp.float32)
        return carry

    lax.fori_loop(0, rows // 16, widen, 0)

    for v in range(2):
        for d in range(1, SIDE):
            rs_copy(v, d).wait_send()
            ag_copy(v, d).wait_send()
            sum_copy(v, d).wait_send()
        for one in plane_copies(v):
            one.wait_send()
    swap.wait_send()
    forward.wait_send()

    @pl.when(c != r)
    def _():
        copy(
            grad_send.at[mine, :], relay, out_send.at[1], out_recv.at[1], near(2)
        ).wait_send()

    @pl.when(flip != r)
    def _():
        copy(half_in, relay, out_send.at[2], out_recv.at[2], near(2)).wait_send()


def gram_gradients(norm_a, norm_b, own_a, own_b, stats):
    images, width = norm_a.shape
    rows = images // SIDE
    half = rows // 2
    whole = pl.BlockSpec(memory_space=pltpu.VMEM)
    out = jax.ShapeDtypeStruct((rows, width), jnp.float32)
    bf16, f32 = jnp.bfloat16, jnp.float32
    dma = pltpu.SemaphoreType.DMA
    return pl.pallas_call(
        functools.partial(gram_kernel, images),
        out_shape=(out, out),
        in_specs=[whole] * 5,
        out_specs=(whole, whole),
        scratch_shapes=[
            pltpu.VMEM((2, 2 * rows + half, rows), bf16),
            pltpu.VMEM((2, SIDE - 1, (2 * rows + half) // SIDE, rows), bf16),
            pltpu.VMEM((2, 2 * rows + half, rows), bf16),
            pltpu.VMEM((2, rows, rows), bf16),
            pltpu.VMEM((2, half, rows), bf16),
            pltpu.VMEM((SIDE, rows, rows), bf16),
            pltpu.VMEM((1, width), f32),
            pltpu.VMEM((2, 8, width), f32),
            pltpu.VMEM((2, SIDE - 1, 8, width), f32),
            pltpu.VMEM((rows, width), bf16),
            pltpu.VMEM((half, width), bf16),
            pltpu.VMEM((half, width), bf16),
            pltpu.VMEM((rows, width), bf16),
            dma((2, SIDE - 1)),
            dma((2, SIDE - 1)),
            dma((2, SIDE - 1)),
            dma((2, SIDE - 1)),
            dma((2, 2)),
            dma((2, 2)),
            dma((2, SIDE - 1)),
            dma((2, SIDE - 1)),
            dma((4,)),
            dma((4,)),
            dma,
        ],
        compiler_params=pltpu.CompilerParams(
            collective_id=0, has_side_effects=True, vmem_limit_bytes=60 * 2**20
        ),
    )(norm_a, norm_b, own_a, own_b, stats)


def standardize_parts(full_view):
    values = full_view.astype(jnp.float32)
    images = values.shape[0]
    column_mean = jnp.sum(values, axis=0) / images
    centered = values - column_mean
    scale = lax.rsqrt(jnp.sum(centered * centered, axis=0) / images + EPSILON)
    return ((centered * scale).astype(jnp.bfloat16), column_mean, scale)


def per_device_gram(view_a, view_b):
    swap = [(r * SIDE + c, c * SIDE + r) for r in range(SIDE) for c in range(SIDE)]
    view_b = lax.ppermute(view_b, ("row", "col"), swap)
    full_a = lax.all_gather(view_a, "col", axis=0, tiled=True)
    full_b = lax.all_gather(view_b, "col", axis=0, tiled=True)
    norm_a, mean_a, scale_a = standardize_parts(full_a)
    norm_b, mean_b, scale_b = standardize_parts(full_b)
    zero = jnp.zeros_like(mean_a)
    stats = jnp.stack([mean_a, scale_a, mean_b, scale_b, zero, zero, zero, zero])
    return gram_gradients(norm_a, norm_b, view_a, view_b, stats)


def solution(mesh):
    square = mesh.shape["row"] == SIDE and mesh.shape["col"] == SIDE
    per_device = per_device_gram if square else per_device_corr
    return jax.shard_map(
        per_device,
        mesh=mesh,
        in_specs=(P(("groups", "col"), "row"), P(("groups", "row"), "col")),
        out_specs=(P(("groups", "col"), "row"), P(("groups", "row"), "col")),
        check_vma=False,
    )
```

```python
import functools

import jax
import jax.numpy as jnp
from jax import lax
from jax.experimental import pallas as pl
from jax.experimental.pallas import tpu as pltpu
from jax.sharding import PartitionSpec as P

EPSILON = 1e-05
OFF_WEIGHT = 0.0051


def standardize(full_view):
    values = full_view.astype(jnp.float32)
    images = values.shape[0]
    column_mean = jnp.sum(values, axis=0) / images
    centered = values - column_mean
    variance = jnp.sum(centered * centered, axis=0) / images
    scale = lax.rsqrt(variance + EPSILON)
    unit_full = centered * scale
    return (unit_full, unit_full.astype(jnp.bfloat16), scale)


def per_device_corr(view_a, view_b):
    rows_a, width_a = view_a.shape
    rows_b, width_b = view_b.shape
    col_count = lax.axis_size("col")
    row_index = lax.axis_index("row")
    col_index = lax.axis_index("col")
    full_a = lax.all_gather(view_a, "col", axis=0, tiled=True)
    full_b = lax.all_gather(view_b, "row", axis=0, tiled=True)
    images = full_a.shape[0]
    unit_a, norm_a, scale_a = standardize(full_a)
    unit_b, norm_b, scale_b = standardize(full_b)
    correlation = (
        lax.dot_general(
            norm_a, norm_b, (((0,), (0,)), ((), ())), preferred_element_type=jnp.float32
        )
        / images
    )
    row_ids = row_index * width_a + jnp.arange(width_a)
    col_ids = col_index * width_b + jnp.arange(width_b)
    on_diagonal = row_ids[:, None] == col_ids[None, :]
    grad_corr = jnp.where(
        on_diagonal, 2.0 * (correlation - 1.0), 2.0 * OFF_WEIGHT * correlation
    ).astype(jnp.bfloat16)
    slab = norm_b
    back_a = lax.psum_scatter(
        lax.dot_general(
            slab, grad_corr, (((1,), (1,)), ((), ())), preferred_element_type=jnp.float32
        ),
        "col",
        scatter_dimension=0,
        tiled=True,
    )
    own_a = lax.dynamic_slice_in_dim(unit_a, col_index * rows_a, rows_a, 0)
    sums_a = jnp.stack([jnp.sum(back_a, axis=0), jnp.sum(back_a * own_a, axis=0)])
    slab = norm_a
    back_b = lax.psum_scatter(
        jnp.dot(slab, grad_corr, preferred_element_type=jnp.float32),
        "row",
        scatter_dimension=0,
        tiled=True,
    )
    own_b = lax.dynamic_slice_in_dim(unit_b, row_index * rows_b, rows_b, 0)
    sums_b = jnp.stack([jnp.sum(back_b, axis=0), jnp.sum(back_b * own_b, axis=0)])
    whole_width = width_b * col_count
    placed_b = lax.dynamic_update_slice(
        jnp.zeros((2, whole_width), jnp.float32), sums_b, (0, col_index * width_b)
    )
    placed_a = lax.dynamic_update_slice(
        jnp.zeros((2, whole_width), jnp.float32), sums_a, (0, row_index * width_a)
    )
    stacked = jnp.concatenate([placed_a, placed_b], axis=0)
    totals = lax.psum(stacked, ("row", "col"))
    total_b = lax.dynamic_slice_in_dim(totals[-2:], col_index * width_b, width_b, 1)
    total_a = lax.dynamic_slice_in_dim(totals[0:2], row_index * width_a, width_a, 1)
    grad_a = scale_a * (back_a - total_a[0] / images - own_a * (total_a[1] / images))
    grad_b = scale_b * (back_b - total_b[0] / images - own_b * (total_b[1] / images))
    return (grad_a, grad_b)


MESH = pl.DeviceIdType.MESH
SIDE = 4
TILE = 256


def gram_kernel(
    images,
    xa,
    raw_b,
    ga,
    gb,
    na,
    nb,
    xb,
    stats,
    half_b,
    part,
    landed,
    gram,
    next_row,
    cross,
    band,
    direct,
    sums,
    sums_in,
    grad_send,
    half_in,
    relay,
    final,
    rs_send,
    rs_recv,
    ag_send,
    ag_recv,
    plane_send,
    plane_recv,
    sum_send,
    sum_recv,
    out_send,
    out_recv,
    a_send,
    a_recv,
    b_send,
    b_recv,
    bg_send,
    bg_recv,
    local_sem,
    own_sem,
):
    g = lax.axis_index("groups")
    r = lax.axis_index("row")
    c = lax.axis_index("col")
    rows, width = xa.shape
    half = rows // 2
    chunk = part.shape[1] // SIDE
    x = c // 2
    lo = c % 2
    flip = (c + 2) % SIDE
    meet = 2 * x + r % 2
    weight = 2.0 * OFF_WEIGHT
    own = pl.ds(pl.multiple_of(c * rows, rows), rows)
    mine = pl.ds(pl.multiple_of(x * half, half), half)
    theirs = pl.ds(pl.multiple_of((1 - x) * half, half), half)
    straight = r // 2 == x
    sibling = (g, r, c + 1 - 2 * lo)
    norms, raws, backs = (na, nb), (xa, xb), (ga, gb)

    def near(d):
        return (g, r, (c + d) % SIDE)

    def far(d):
        return (g, (r + d) % SIDE, c)

    def copy(src, dst, send, recv, to):
        return pltpu.make_async_remote_copy(
            src_ref=src,
            dst_ref=dst,
            send_sem=send,
            recv_sem=recv,
            device_id=to,
            device_id_type=MESH,
        )

    barrier = pltpu.get_barrier_semaphore()
    for d in range(1, SIDE):
        pl.semaphore_signal(barrier, inc=1, device_id=near(d), device_id_type=MESH)
        pl.semaphore_signal(barrier, inc=1, device_id=far(d), device_id_type=MESH)
    odd = (r + c) % 2 == 1

    @pl.when(odd)
    def _():
        for plane in (c, flip):
            pl.semaphore_signal(
                barrier, inc=1, device_id=(g, plane, meet), device_id_type=MESH
            )
        pl.semaphore_wait(barrier, 2 * SIDE)

    @pl.when(jnp.logical_not(odd))
    def _():
        pl.semaphore_wait(barrier, 2 * (SIDE - 1))

    def chunk_at(owner):
        return pl.ds(pl.multiple_of(owner * chunk, 16), chunk)

    def make_part(v):
        norm = norms[v]

        def body(i, carry):
            left = jnp.where(i < 4, c * rows + (i % 2) * half, lo * rows + x * half)
            right = jnp.where(i < 2, c, jnp.where(i < 4, (c + 1) % SIDE, lo + 2)) * rows
            a = norm[pl.ds(pl.multiple_of(left, half), half), :]
            b = norm[pl.ds(pl.multiple_of(right, rows), rows), :]
            t = lax.dot_general(
                a, b, (((1,), (1,)), ((), ())), preferred_element_type=jnp.float32
            )
            part[v, pl.ds(pl.multiple_of(i * half, half), half), :] = t.astype(jnp.bfloat16)
            return carry

        lax.fori_loop(0, 5, body, 0)

    def rs_copy(v, d):
        owner = (r + d) % SIDE
        return copy(
            part.at[v, chunk_at(owner), :],
            landed.at[v, d - 1],
            rs_send.at[v, d - 1],
            rs_recv.at[v, d - 1],
            far(d),
        )

    def ag_copy(v, d):
        return copy(
            gram.at[v, chunk_at(r), :],
            gram.at[v, chunk_at(r), :],
            ag_send.at[v, d - 1],
            ag_recv.at[v, d - 1],
            far(d),
        )

    def ag_arrival(v, d):
        owner = (r + SIDE - d) % SIDE
        return copy(
            gram.at[v, chunk_at(owner), :],
            gram.at[v, chunk_at(owner), :],
            ag_send.at[v, d - 1],
            ag_recv.at[v, d - 1],
            far(d),
        )

    def reduce(v):
        for d in range(1, SIDE):
            rs_copy(v, d).wait_recv()
        total = part[v, chunk_at(r), :].astype(jnp.float32)
        for d in range(1, SIDE):
            total = total + landed[v, d - 1].astype(jnp.float32)
        gram[v, chunk_at(r), :] = total.astype(jnp.bfloat16)
        for d in range(1, SIDE):
            ag_copy(v, d).start()

    def plane_copies(v):
        return (
            copy(
                gram.at[v, pl.ds(rows, rows), :],
                next_row.at[v],
                plane_send.at[v, 0],
                plane_recv.at[v, 0],
                near(1),
            ),
            copy(
                gram.at[v, pl.ds(2 * rows, half), :],
                cross.at[v],
                plane_send.at[v, 1],
                plane_recv.at[v, 1],
                near(2),
            ),
        )

    def share(v):
        for d in range(1, SIDE):
            ag_arrival(v, d).wait_recv()
        for one in plane_copies(v):
            one.start()

    def turned(block):
        return block.astype(jnp.float32).T.astype(jnp.bfloat16)

    def make_band(v):
        for one in plane_copies(v):
            one.wait_recv()
        band[c] = gram[v, pl.ds(0, rows), :]
        band[(c + 1) % SIDE] = gram[v, pl.ds(rows, rows), :]
        band[(c + 3) % SIDE] = turned(next_row[v])

        @pl.when(x == 0)
        def _():
            band[flip, pl.ds(0, half), :] = gram[v, pl.ds(2 * rows, half), :]
            band[flip, pl.ds(half, half), :] = cross[v]

        @pl.when(x == 1)
        def _():
            band[flip, :, pl.ds(0, half)] = turned(cross[v])
            band[flip, :, pl.ds(half, half)] = turned(gram[v, pl.ds(2 * rows, half), :])

    def unit_of(w, columns):
        mean = stats[pl.ds(2 * w, 1), columns]
        scale = stats[pl.ds(2 * w + 1, 1), columns]
        return (raws[w][:, columns].astype(jnp.float32) - mean) * scale, scale

    def sum_copy(w, d):
        return copy(
            sums.at[w],
            sums_in.at[w, d - 1],
            sum_send.at[w, d - 1],
            sum_recv.at[w, d - 1],
            near(d),
        )

    def make_back(w):
        norm, other, back_ref = norms[w], norms[1 - w], backs[w]

        def body(j, carry):
            columns = pl.ds(pl.multiple_of(j * TILE, TILE), TILE)
            mixed = jnp.zeros((rows, TILE), jnp.float32)
            for block in range(SIDE):
                mixed = mixed + jnp.dot(
                    band[block],
                    norm[pl.ds(block * rows, rows), columns],
                    preferred_element_type=jnp.float32,
                )
            term = direct[:, columns] * other[own, columns].astype(jnp.float32)
            back = (weight / images) * mixed + term
            unit, _ = unit_of(w, columns)
            back_ref[:, columns] = back
            sums[w, pl.ds(0, 1), columns] = jnp.sum(back, axis=0, keepdims=True)
            sums[w, pl.ds(1, 1), columns] = jnp.sum(back * unit, axis=0, keepdims=True)
            return carry

        lax.fori_loop(0, width // TILE, body, 0)
        for d in range(1, SIDE):
            sum_copy(w, d).start()

    def make_grad(w, target):
        for d in range(1, SIDE):
            sum_copy(w, d).wait_recv()

        def body(j, carry):
            columns = pl.ds(pl.multiple_of(j * TILE, TILE), TILE)
            total = sums[w, pl.ds(0, 2), columns]
            for d in range(1, SIDE):
                total = total + sums_in[w, d - 1, pl.ds(0, 2), columns]
            total = total / images
            unit, scale = unit_of(w, columns)
            grad = scale * (backs[w][:, columns] - total[0:1] - unit * total[1:2])
            target[:, columns] = grad.astype(target.dtype)
            return carry

        lax.fori_loop(0, width // TILE, body, 0)

    def make_direct():
        def body(i, acc):
            lines = pl.ds(pl.multiple_of(i * 16, 16), 16)
            prod = na[lines, :].astype(jnp.float32) * nb[lines, :].astype(jnp.float32)
            return acc + prod[0:8] + prod[8:16]

        acc = lax.fori_loop(0, images // 16, body, jnp.zeros((8, width), jnp.float32))
        diagonal = jnp.sum(acc, axis=0, keepdims=True) / images
        rounded = (2.0 * (diagonal - 1.0)).astype(jnp.bfloat16).astype(jnp.float32)
        direct[...] = rounded - weight * diagonal

    def block_of(b):
        return pl.ds(pl.multiple_of(b * rows, rows), rows)

    def half_of(b, h):
        return pl.ds(pl.multiple_of(b * rows + h * half, half), half)

    def lines_of(i):
        return pl.ds(pl.multiple_of(i * 32, 32), 32)

    def fold(values):
        return values[0:8] + values[8:16] + values[16:24] + values[24:32]

    def standardize_in_place(w):
        norm = norms[w]
        zero = jnp.zeros((8, width), jnp.float32)

        def add(i, acc):
            return acc + fold(norm[lines_of(i), :].astype(jnp.float32))

        acc = lax.fori_loop(0, images // 32, add, zero)
        mean = jnp.sum(acc, axis=0, keepdims=True) / images
        stats[pl.ds(2 * w, 1), :] = mean

        def add_square(i, acc):
            centered = norm[lines_of(i), :].astype(jnp.float32) - stats[pl.ds(2 * w, 1), :]
            return acc + fold(centered * centered)

        acc = lax.fori_loop(0, images // 32, add_square, zero)
        variance = jnp.sum(acc, axis=0, keepdims=True) / images
        stats[pl.ds(2 * w + 1, 1), :] = lax.rsqrt(variance + EPSILON)

        def write(i, carry):
            centered = norm[lines_of(i), :].astype(jnp.float32) - stats[pl.ds(2 * w, 1), :]
            unit = centered * stats[pl.ds(2 * w + 1, 1), :]
            norm[lines_of(i), :] = unit.astype(jnp.bfloat16)
            return carry

        lax.fori_loop(0, images // 32, write, 0)

    sums[...] = jnp.zeros_like(sums)

    a_side = copy(xa, na.at[own, :], a_send.at[0], a_recv.at[0], sibling)
    a_cross = copy(xa, na.at[own, :], a_send.at[1], a_recv.at[1], near(2))
    a_pass = copy(
        na.at[block_of(flip), :],
        na.at[block_of(flip), :],
        a_send.at[2],
        a_recv.at[2],
        sibling,
    )
    a_own = pltpu.make_async_copy(xa, na.at[own, :], own_sem)
    b_swap = copy(raw_b.at[theirs, :], half_b, b_send.at[0], b_recv.at[0], near(2))
    b_place = nb.at[half_of(r, x), :]

    def b_hop(src, plane, send):
        @pl.when(straight)
        def _():
            copy(
                src, b_place, b_send.at[send], b_recv.at[1], (g, plane, meet)
            ).start()

        @pl.when(jnp.logical_not(straight))
        def _():
            copy(
                src, b_place, b_send.at[send], b_recv.at[2], (g, plane, meet)
            ).start()

    b_swap.start()
    a_side.start()
    a_own.start()

    @pl.when(c != r)
    def _():
        b_hop(raw_b.at[mine, :], c, 1)

    @pl.when(c == r)
    def _():
        stay = pltpu.make_async_copy(raw_b.at[mine, :], b_place, local_sem)
        stay.start()
        stay.wait()

    b_swap.wait_recv()
    a_cross.start()

    @pl.when(flip != r)
    def _():
        b_hop(half_b, flip, 2)

    @pl.when(flip == r)
    def _():
        stay = pltpu.make_async_copy(half_b, b_place, local_sem)
        stay.start()
        stay.wait()

    a_cross.wait_recv()
    a_pass.start()

    def b_spread(k):
        block = c if k == 0 else flip
        here = nb.at[half_of(block, x), :]
        came = nb.at[half_of(flip if k == 0 else c, 1 - x), :]
        return (
            copy(here, here, bg_send.at[k, 0], bg_recv.at[k, 0], sibling),
            copy(here, here, bg_send.at[k, 1], bg_recv.at[k, 1], near(2)),
            copy(came, came, bg_send.at[k, 2], bg_recv.at[k, 2], sibling),
        )

    @pl.when(c != r)
    def _():
        here = nb.at[half_of(c, x), :]
        copy(here, here, b_send.at[1], b_recv.at[1], near(2)).wait_recv()

    b_spread(0)[1].start()
    b_spread(0)[0].start()

    @pl.when(flip != r)
    def _():
        here = nb.at[half_of(flip, x), :]
        copy(here, here, b_send.at[2], b_recv.at[2], near(2)).wait_recv()

    b_spread(1)[1].start()
    b_spread(1)[0].start()

    other_col = c + 1 - 2 * lo
    far_col = (other_col + 2) % SIDE

    def arrived(ref, place, recv):
        copy(ref.at[place, :], ref.at[place, :], a_send.at[0], recv, near(2)).wait_recv()

    a_own.wait()
    arrived(na, block_of(other_col), a_recv.at[0])
    arrived(na, block_of(far_col), a_recv.at[2])
    a_side.wait_send()
    a_cross.wait_send()
    a_pass.wait_send()
    standardize_in_place(0)
    make_part(0)
    for d in range(1, SIDE):
        rs_copy(0, d).start()
    reduce(0)

    for k in range(2):
        arrived(nb, half_of(flip if k == 0 else c, 1 - x), bg_recv.at[k, 1])
        b_spread(k)[2].start()
    for k in range(2):
        arrived(nb, half_of(other_col if k == 0 else far_col, x), bg_recv.at[k, 0])
        arrived(nb, half_of(far_col if k == 0 else other_col, 1 - x), bg_recv.at[k, 2])
    for k in range(2):
        for one in b_spread(k):
            one.wait_send()
    keep = pltpu.make_async_copy(nb.at[own, :], xb, local_sem)
    keep.start()
    keep.wait()
    standardize_in_place(1)
    make_part(1)
    for d in range(1, SIDE):
        rs_copy(1, d).start()
    make_direct()
    share(0)
    make_band(0)
    make_back(1)
    reduce(1)
    make_grad(1, grad_send)

    swap = copy(
        grad_send.at[theirs, :], half_in, out_send.at[0], out_recv.at[0], near(2)
    )
    swap.start()

    def hop(src, plane, send):
        @pl.when(straight)
        def _():
            copy(
                src, final.at[mine, :], out_send.at[send], out_recv.at[1], (g, plane, meet)
            ).start()

        @pl.when(jnp.logical_not(straight))
        def _():
            copy(src, relay, out_send.at[send], out_recv.at[2], (g, plane, meet)).start()

    @pl.when(c != r)
    def _():
        hop(grad_send.at[mine, :], c, 1)

    @pl.when(c == r)
    def _():
        stay = pltpu.make_async_copy(grad_send.at[mine, :], final.at[mine, :], local_sem)
        stay.start()
        stay.wait()

    swap.wait_recv()

    @pl.when(flip != r)
    def _():
        hop(half_in, flip, 2)

    @pl.when(flip == r)
    def _():
        stay = pltpu.make_async_copy(half_in, relay, local_sem)
        stay.start()
        stay.wait()

    share(1)
    make_band(1)
    make_back(0)
    make_grad(0, ga)

    forward = copy(relay, final.at[mine, :], out_send.at[3], out_recv.at[3], near(2))

    @pl.when(flip != r)
    def _():
        copy(half_in, relay, out_send.at[2], out_recv.at[2], near(2)).wait_recv()

    forward.start()

    @pl.when(c != r)
    def _():
        copy(
            half_in, final.at[mine, :], out_send.at[1], out_recv.at[1], near(2)
        ).wait_recv()

    copy(relay, final.at[theirs, :], out_send.at[3], out_recv.at[3], near(2)).wait_recv()

    def widen(i, carry):
        lines = pl.ds(pl.multiple_of(i * 16, 16), 16)
        gb[lines, :] = final[lines, :].astype(jnp.float32)
        return carry

    lax.fori_loop(0, rows // 16, widen, 0)

    for v in range(2):
        for d in range(1, SIDE):
            rs_copy(v, d).wait_send()
            ag_copy(v, d).wait_send()
            sum_copy(v, d).wait_send()
        for one in plane_copies(v):
            one.wait_send()
    b_swap.wait_send()
    swap.wait_send()
    forward.wait_send()

    @pl.when(c != r)
    def _():
        copy(
            grad_send.at[mine, :], relay, out_send.at[1], out_recv.at[1], near(2)
        ).wait_send()
        copy(raw_b.at[mine, :], half_b, b_send.at[1], b_recv.at[1], near(2)).wait_send()

    @pl.when(flip != r)
    def _():
        copy(half_in, relay, out_send.at[2], out_recv.at[2], near(2)).wait_send()
        copy(half_b, half_in, b_send.at[2], b_recv.at[2], near(2)).wait_send()


def gram_gradients(view_a, view_b):
    rows, width = view_a.shape
    images = SIDE * rows
    half = rows // 2
    whole = pl.BlockSpec(memory_space=pltpu.VMEM)
    out = jax.ShapeDtypeStruct((rows, width), jnp.float32)
    bf16, f32 = jnp.bfloat16, jnp.float32
    dma = pltpu.SemaphoreType.DMA
    return pl.pallas_call(
        functools.partial(gram_kernel, images),
        out_shape=(out, out),
        in_specs=[whole] * 2,
        out_specs=(whole, whole),
        scratch_shapes=[
            pltpu.VMEM((images, width), bf16),
            pltpu.VMEM((images, width), bf16),
            pltpu.VMEM((rows, width), bf16),
            pltpu.VMEM((8, width), f32),
            pltpu.VMEM((half, width), bf16),
            pltpu.VMEM((2, 2 * rows + half, rows), bf16),
            pltpu.VMEM((2, SIDE - 1, (2 * rows + half) // SIDE, rows), bf16),
            pltpu.VMEM((2, 2 * rows + half, rows), bf16),
            pltpu.VMEM((2, rows, rows), bf16),
            pltpu.VMEM((2, half, rows), bf16),
            pltpu.VMEM((SIDE, rows, rows), bf16),
            pltpu.VMEM((1, width), f32),
            pltpu.VMEM((2, 8, width), f32),
            pltpu.VMEM((2, SIDE - 1, 8, width), f32),
            pltpu.VMEM((rows, width), bf16),
            pltpu.VMEM((half, width), bf16),
            pltpu.VMEM((half, width), bf16),
            pltpu.VMEM((rows, width), bf16),
            dma((2, SIDE - 1)),
            dma((2, SIDE - 1)),
            dma((2, SIDE - 1)),
            dma((2, SIDE - 1)),
            dma((2, 2)),
            dma((2, 2)),
            dma((2, SIDE - 1)),
            dma((2, SIDE - 1)),
            dma((4,)),
            dma((4,)),
            dma((3,)),
            dma((3,)),
            dma((3,)),
            dma((3,)),
            dma((2, 3)),
            dma((2, 3)),
            dma,
            dma,
        ],
        compiler_params=pltpu.CompilerParams(
            collective_id=1, has_side_effects=True, vmem_limit_bytes=60 * 2**20
        ),
    )(view_a, view_b)


def solution(mesh):
    square = mesh.shape["row"] == SIDE and mesh.shape["col"] == SIDE
    per_device = gram_gradients if square else per_device_corr
    return jax.shard_map(
        per_device,
        mesh=mesh,
        in_specs=(P(("groups", "col"), "row"), P(("groups", "row"), "col")),
        out_specs=(P(("groups", "col"), "row"), P(("groups", "row"), "col")),
        check_vma=False,
    )
```

```python
import functools

import jax
import jax.numpy as jnp
from jax import lax
from jax.experimental import pallas as pl
from jax.experimental.pallas import tpu as pltpu
from jax.sharding import PartitionSpec as P

EPSILON = 1e-05
OFF_WEIGHT = 0.0051


def standardize(full_view):
    values = full_view.astype(jnp.float32)
    images = values.shape[0]
    column_mean = jnp.sum(values, axis=0) / images
    centered = values - column_mean
    variance = jnp.sum(centered * centered, axis=0) / images
    scale = lax.rsqrt(variance + EPSILON)
    unit_full = centered * scale
    return (unit_full, unit_full.astype(jnp.bfloat16), scale)


def per_device_corr(view_a, view_b):
    rows_a, width_a = view_a.shape
    rows_b, width_b = view_b.shape
    col_count = lax.axis_size("col")
    row_index = lax.axis_index("row")
    col_index = lax.axis_index("col")
    full_a = lax.all_gather(view_a, "col", axis=0, tiled=True)
    full_b = lax.all_gather(view_b, "row", axis=0, tiled=True)
    images = full_a.shape[0]
    unit_a, norm_a, scale_a = standardize(full_a)
    unit_b, norm_b, scale_b = standardize(full_b)
    correlation = (
        lax.dot_general(
            norm_a, norm_b, (((0,), (0,)), ((), ())), preferred_element_type=jnp.float32
        )
        / images
    )
    row_ids = row_index * width_a + jnp.arange(width_a)
    col_ids = col_index * width_b + jnp.arange(width_b)
    on_diagonal = row_ids[:, None] == col_ids[None, :]
    grad_corr = jnp.where(
        on_diagonal, 2.0 * (correlation - 1.0), 2.0 * OFF_WEIGHT * correlation
    ).astype(jnp.bfloat16)
    slab = norm_b
    back_a = lax.psum_scatter(
        lax.dot_general(
            slab, grad_corr, (((1,), (1,)), ((), ())), preferred_element_type=jnp.float32
        ),
        "col",
        scatter_dimension=0,
        tiled=True,
    )
    own_a = lax.dynamic_slice_in_dim(unit_a, col_index * rows_a, rows_a, 0)
    sums_a = jnp.stack([jnp.sum(back_a, axis=0), jnp.sum(back_a * own_a, axis=0)])
    slab = norm_a
    back_b = lax.psum_scatter(
        jnp.dot(slab, grad_corr, preferred_element_type=jnp.float32),
        "row",
        scatter_dimension=0,
        tiled=True,
    )
    own_b = lax.dynamic_slice_in_dim(unit_b, row_index * rows_b, rows_b, 0)
    sums_b = jnp.stack([jnp.sum(back_b, axis=0), jnp.sum(back_b * own_b, axis=0)])
    whole_width = width_b * col_count
    placed_b = lax.dynamic_update_slice(
        jnp.zeros((2, whole_width), jnp.float32), sums_b, (0, col_index * width_b)
    )
    placed_a = lax.dynamic_update_slice(
        jnp.zeros((2, whole_width), jnp.float32), sums_a, (0, row_index * width_a)
    )
    stacked = jnp.concatenate([placed_a, placed_b], axis=0)
    totals = lax.psum(stacked, ("row", "col"))
    total_b = lax.dynamic_slice_in_dim(totals[-2:], col_index * width_b, width_b, 1)
    total_a = lax.dynamic_slice_in_dim(totals[0:2], row_index * width_a, width_a, 1)
    grad_a = scale_a * (back_a - total_a[0] / images - own_a * (total_a[1] / images))
    grad_b = scale_b * (back_b - total_b[0] / images - own_b * (total_b[1] / images))
    return (grad_a, grad_b)


MESH = pl.DeviceIdType.MESH
SIDE = 4
TILE = 256


def gram_kernel(
    images,
    xa,
    raw_b,
    ga,
    gb,
    na,
    nb,
    xb,
    stats,
    half_b,
    back_b,
    part,
    landed,
    gram,
    next_row,
    cross,
    band,
    direct,
    sums,
    sums_in,
    grad_send,
    half_in,
    relay,
    final,
    rs_send,
    rs_recv,
    ag_send,
    ag_recv,
    plane_send,
    plane_recv,
    sum_send,
    sum_recv,
    out_send,
    out_recv,
    a_send,
    a_recv,
    b_send,
    b_recv,
    bg_send,
    bg_recv,
    local_sem,
    own_sem,
):
    g = lax.axis_index("groups")
    r = lax.axis_index("row")
    c = lax.axis_index("col")
    rows, width = xa.shape
    half = rows // 2
    chunk = part.shape[1] // SIDE
    x = c // 2
    lo = c % 2
    flip = (c + 2) % SIDE
    meet = 2 * x + r % 2
    weight = 2.0 * OFF_WEIGHT
    own = pl.ds(pl.multiple_of(c * rows, rows), rows)
    mine = pl.ds(pl.multiple_of(x * half, half), half)
    theirs = pl.ds(pl.multiple_of((1 - x) * half, half), half)
    straight = r // 2 == x
    sibling = (g, r, c + 1 - 2 * lo)
    norms, raws, backs = (na, nb), (xa, xb), (ga, back_b)

    def near(d):
        return (g, r, (c + d) % SIDE)

    def far(d):
        return (g, (r + d) % SIDE, c)

    def copy(src, dst, send, recv, to):
        return pltpu.make_async_remote_copy(
            src_ref=src,
            dst_ref=dst,
            send_sem=send,
            recv_sem=recv,
            device_id=to,
            device_id_type=MESH,
        )

    barrier = pltpu.get_barrier_semaphore()
    for d in range(1, SIDE):
        pl.semaphore_signal(barrier, inc=1, device_id=near(d), device_id_type=MESH)
        pl.semaphore_signal(barrier, inc=1, device_id=far(d), device_id_type=MESH)
    odd = (r + c) % 2 == 1

    @pl.when(odd)
    def _():
        for plane in (c, flip):
            pl.semaphore_signal(
                barrier, inc=1, device_id=(g, plane, meet), device_id_type=MESH
            )
        pl.semaphore_wait(barrier, 2 * SIDE)

    @pl.when(jnp.logical_not(odd))
    def _():
        pl.semaphore_wait(barrier, 2 * (SIDE - 1))

    def chunk_at(owner):
        return pl.ds(pl.multiple_of(owner * chunk, 16), chunk)

    def make_part(v):
        norm = norms[v]

        def body(i, carry):
            left = jnp.where(i < 4, c * rows + (i % 2) * half, lo * rows + x * half)
            right = jnp.where(i < 2, c, jnp.where(i < 4, (c + 1) % SIDE, lo + 2)) * rows
            a = norm[pl.ds(pl.multiple_of(left, half), half), :]
            b = norm[pl.ds(pl.multiple_of(right, rows), rows), :]
            t = lax.dot_general(
                a, b, (((1,), (1,)), ((), ())), preferred_element_type=jnp.float32
            )
            part[v, pl.ds(pl.multiple_of(i * half, half), half), :] = t.astype(jnp.bfloat16)
            return carry

        lax.fori_loop(0, 5, body, 0)

    def rs_copy(v, d):
        owner = (r + d) % SIDE
        return copy(
            part.at[v, chunk_at(owner), :],
            landed.at[v, d - 1],
            rs_send.at[v, d - 1],
            rs_recv.at[v, d - 1],
            far(d),
        )

    def ag_copy(v, d):
        return copy(
            gram.at[v, chunk_at(r), :],
            gram.at[v, chunk_at(r), :],
            ag_send.at[v, d - 1],
            ag_recv.at[v, d - 1],
            far(d),
        )

    def ag_arrival(v, d):
        owner = (r + SIDE - d) % SIDE
        return copy(
            gram.at[v, chunk_at(owner), :],
            gram.at[v, chunk_at(owner), :],
            ag_send.at[v, d - 1],
            ag_recv.at[v, d - 1],
            far(d),
        )

    def reduce(v):
        for d in range(1, SIDE):
            rs_copy(v, d).wait_recv()
        total = part[v, chunk_at(r), :].astype(jnp.float32)
        for d in range(1, SIDE):
            total = total + landed[v, d - 1].astype(jnp.float32)
        gram[v, chunk_at(r), :] = total.astype(jnp.bfloat16)
        for d in range(1, SIDE):
            ag_copy(v, d).start()

    def plane_copies(v):
        return (
            copy(
                gram.at[v, pl.ds(rows, rows), :],
                next_row.at[v],
                plane_send.at[v, 0],
                plane_recv.at[v, 0],
                near(1),
            ),
            copy(
                gram.at[v, pl.ds(2 * rows, half), :],
                cross.at[v],
                plane_send.at[v, 1],
                plane_recv.at[v, 1],
                near(2),
            ),
        )

    def share(v):
        for d in range(1, SIDE):
            ag_arrival(v, d).wait_recv()
        for one in plane_copies(v):
            one.start()

    def turned(block):
        return block.astype(jnp.float32).T.astype(jnp.bfloat16)

    def make_band(v):
        for one in plane_copies(v):
            one.wait_recv()
        band[c] = gram[v, pl.ds(0, rows), :]
        band[(c + 1) % SIDE] = gram[v, pl.ds(rows, rows), :]
        band[(c + 3) % SIDE] = turned(next_row[v])

        @pl.when(x == 0)
        def _():
            band[flip, pl.ds(0, half), :] = gram[v, pl.ds(2 * rows, half), :]
            band[flip, pl.ds(half, half), :] = cross[v]

        @pl.when(x == 1)
        def _():
            band[flip, :, pl.ds(0, half)] = turned(cross[v])
            band[flip, :, pl.ds(half, half)] = turned(gram[v, pl.ds(2 * rows, half), :])

    def unit_of(w, columns):
        mean = stats[pl.ds(2 * w, 1), columns]
        scale = stats[pl.ds(2 * w + 1, 1), columns]
        return (raws[w][:, columns].astype(jnp.float32) - mean) * scale, scale

    def sum_copy(w, d):
        return copy(
            sums.at[w],
            sums_in.at[w, d - 1],
            sum_send.at[w, d - 1],
            sum_recv.at[w, d - 1],
            near(d),
        )

    def make_back(w):
        norm, other, back_ref = norms[w], norms[1 - w], backs[w]

        def body(j, carry):
            columns = pl.ds(pl.multiple_of(j * TILE, TILE), TILE)
            mixed = jnp.zeros((rows, TILE), jnp.float32)
            for block in range(SIDE):
                mixed = mixed + jnp.dot(
                    band[block],
                    norm[pl.ds(block * rows, rows), columns],
                    preferred_element_type=jnp.float32,
                )
            term = direct[:, columns] * other[own, columns].astype(jnp.float32)
            back = (weight / images) * mixed + term
            unit, _ = unit_of(w, columns)
            back_ref[:, columns] = back
            sums[w, pl.ds(0, 1), columns] = jnp.sum(back, axis=0, keepdims=True)
            sums[w, pl.ds(1, 1), columns] = jnp.sum(back * unit, axis=0, keepdims=True)
            return carry

        lax.fori_loop(0, width // TILE, body, 0)
        for d in range(1, SIDE):
            sum_copy(w, d).start()

    def make_grad(w, target):
        for d in range(1, SIDE):
            sum_copy(w, d).wait_recv()

        def body(j, carry):
            columns = pl.ds(pl.multiple_of(j * TILE, TILE), TILE)
            total = sums[w, pl.ds(0, 2), columns]
            for d in range(1, SIDE):
                total = total + sums_in[w, d - 1, pl.ds(0, 2), columns]
            total = total / images
            unit, scale = unit_of(w, columns)
            grad = scale * (backs[w][:, columns] - total[0:1] - unit * total[1:2])
            target[:, columns] = grad.astype(target.dtype)
            return carry

        lax.fori_loop(0, width // TILE, body, 0)

    def make_direct():
        def body(i, acc):
            lines = pl.ds(pl.multiple_of(i * 16, 16), 16)
            prod = na[lines, :].astype(jnp.float32) * nb[lines, :].astype(jnp.float32)
            return acc + prod[0:8] + prod[8:16]

        acc = lax.fori_loop(0, images // 16, body, jnp.zeros((8, width), jnp.float32))
        diagonal = jnp.sum(acc, axis=0, keepdims=True) / images
        rounded = (2.0 * (diagonal - 1.0)).astype(jnp.bfloat16).astype(jnp.float32)
        direct[...] = rounded - weight * diagonal

    def block_of(b):
        return pl.ds(pl.multiple_of(b * rows, rows), rows)

    def half_of(b, h):
        return pl.ds(pl.multiple_of(b * rows + h * half, half), half)

    def lines_of(i):
        return pl.ds(pl.multiple_of(i * 32, 32), 32)

    def fold(values):
        return values[0:8] + values[8:16] + values[16:24] + values[24:32]

    def standardize_in_place(w):
        norm = norms[w]
        zero = jnp.zeros((8, width), jnp.float32)

        def add(i, acc):
            return acc + fold(norm[lines_of(i), :].astype(jnp.float32))

        acc = lax.fori_loop(0, images // 32, add, zero)
        mean = jnp.sum(acc, axis=0, keepdims=True) / images
        stats[pl.ds(2 * w, 1), :] = mean

        def add_square(i, acc):
            centered = norm[lines_of(i), :].astype(jnp.float32) - stats[pl.ds(2 * w, 1), :]
            return acc + fold(centered * centered)

        acc = lax.fori_loop(0, images // 32, add_square, zero)
        variance = jnp.sum(acc, axis=0, keepdims=True) / images
        stats[pl.ds(2 * w + 1, 1), :] = lax.rsqrt(variance + EPSILON)

        def write(i, carry):
            centered = norm[lines_of(i), :].astype(jnp.float32) - stats[pl.ds(2 * w, 1), :]
            unit = centered * stats[pl.ds(2 * w + 1, 1), :]
            norm[lines_of(i), :] = unit.astype(jnp.bfloat16)
            return carry

        lax.fori_loop(0, images // 32, write, 0)

    sums[...] = jnp.zeros_like(sums)

    a_side = copy(xa, na.at[own, :], a_send.at[0], a_recv.at[0], sibling)
    a_cross = copy(xa, na.at[own, :], a_send.at[1], a_recv.at[1], near(2))
    a_pass = copy(
        na.at[block_of(flip), :],
        na.at[block_of(flip), :],
        a_send.at[2],
        a_recv.at[2],
        sibling,
    )
    a_own = pltpu.make_async_copy(xa, na.at[own, :], own_sem)
    b_swap = copy(raw_b.at[theirs, :], half_b, b_send.at[0], b_recv.at[0], near(2))
    b_place = nb.at[half_of(r, x), :]

    def b_hop(src, plane, send):
        @pl.when(straight)
        def _():
            copy(
                src, b_place, b_send.at[send], b_recv.at[1], (g, plane, meet)
            ).start()

        @pl.when(jnp.logical_not(straight))
        def _():
            copy(
                src, b_place, b_send.at[send], b_recv.at[2], (g, plane, meet)
            ).start()

    b_swap.start()
    a_side.start()
    a_own.start()

    @pl.when(c != r)
    def _():
        b_hop(raw_b.at[mine, :], c, 1)

    @pl.when(c == r)
    def _():
        stay = pltpu.make_async_copy(raw_b.at[mine, :], b_place, local_sem)
        stay.start()
        stay.wait()

    b_swap.wait_recv()
    a_cross.start()

    @pl.when(flip != r)
    def _():
        b_hop(half_b, flip, 2)

    @pl.when(flip == r)
    def _():
        stay = pltpu.make_async_copy(half_b, b_place, local_sem)
        stay.start()
        stay.wait()

    a_cross.wait_recv()
    a_pass.start()

    def b_spread(k):
        block = c if k == 0 else flip
        here = nb.at[half_of(block, x), :]
        came = nb.at[half_of(flip if k == 0 else c, 1 - x), :]
        return (
            copy(here, here, bg_send.at[k, 0], bg_recv.at[k, 0], sibling),
            copy(here, here, bg_send.at[k, 1], bg_recv.at[k, 1], near(2)),
            copy(came, came, bg_send.at[k, 2], bg_recv.at[k, 2], sibling),
        )

    @pl.when(c != r)
    def _():
        here = nb.at[half_of(c, x), :]
        copy(here, here, b_send.at[1], b_recv.at[1], near(2)).wait_recv()

    b_spread(0)[1].start()
    b_spread(0)[0].start()

    @pl.when(flip != r)
    def _():
        here = nb.at[half_of(flip, x), :]
        copy(here, here, b_send.at[2], b_recv.at[2], near(2)).wait_recv()

    b_spread(1)[1].start()
    b_spread(1)[0].start()

    other_col = c + 1 - 2 * lo
    far_col = (other_col + 2) % SIDE

    def arrived(ref, place, recv):
        copy(ref.at[place, :], ref.at[place, :], a_send.at[0], recv, near(2)).wait_recv()

    a_own.wait()
    arrived(na, block_of(other_col), a_recv.at[0])
    arrived(na, block_of(far_col), a_recv.at[2])
    a_side.wait_send()
    a_cross.wait_send()
    a_pass.wait_send()
    standardize_in_place(0)
    make_part(0)
    for d in range(1, SIDE):
        rs_copy(0, d).start()
    reduce(0)

    for k in range(2):
        arrived(nb, half_of(flip if k == 0 else c, 1 - x), bg_recv.at[k, 1])
        b_spread(k)[2].start()
    for k in range(2):
        arrived(nb, half_of(other_col if k == 0 else far_col, x), bg_recv.at[k, 0])
        arrived(nb, half_of(far_col if k == 0 else other_col, 1 - x), bg_recv.at[k, 2])
    for k in range(2):
        for one in b_spread(k):
            one.wait_send()
    keep = pltpu.make_async_copy(nb.at[own, :], xb, local_sem)
    keep.start()
    keep.wait()
    standardize_in_place(1)
    make_part(1)
    for d in range(1, SIDE):
        rs_copy(1, d).start()
    make_direct()
    share(0)
    make_band(0)
    make_back(1)
    reduce(1)
    make_grad(1, grad_send)

    quarter = half // 2

    def final_at(h, q):
        return final.at[
            pl.ds(pl.multiple_of(h * half + q * quarter, quarter), quarter), :
        ]

    def mine_at(q):
        return grad_send.at[
            pl.ds(pl.multiple_of(x * half + q * quarter, quarter), quarter), :
        ]

    def relay_at(q):
        return relay.at[pl.ds(q * quarter, quarter), :]

    def half_in_at(q):
        return half_in.at[pl.ds(q * quarter, quarter), :]

    swap = copy(
        grad_send.at[theirs, :], half_in, out_send.at[0, 0], out_recv.at[0, 0], near(2)
    )
    swap.start()

    def hop(src, plane, send):
        to = (g, plane, meet)
        for q in range(2):
            piece = src(q)

            @pl.when(straight)
            def _():
                copy(
                    piece, final_at(x, q), out_send.at[send, q], out_recv.at[1, q], to
                ).start()

            @pl.when(jnp.logical_not(straight))
            def _():
                copy(
                    piece, relay_at(q), out_send.at[send, q], out_recv.at[2, q], to
                ).start()

    @pl.when(c != r)
    def _():
        hop(mine_at, c, 1)

    @pl.when(c == r)
    def _():
        stay = pltpu.make_async_copy(grad_send.at[mine, :], final.at[mine, :], local_sem)
        stay.start()
        stay.wait()

    swap.wait_recv()

    @pl.when(flip != r)
    def _():
        hop(half_in_at, flip, 2)

    @pl.when(flip == r)
    def _():
        stay = pltpu.make_async_copy(half_in, relay, local_sem)
        stay.start()
        stay.wait()

    share(1)
    make_band(1)
    make_back(0)

    def forward(q):
        return copy(
            relay_at(q), final_at(x, q), out_send.at[3, q], out_recv.at[3, q], near(2)
        )

    def pass_on(q):
        @pl.when(flip != r)
        def _():
            copy(
                relay_at(q), relay_at(q), out_send.at[2, q], out_recv.at[2, q], near(2)
            ).wait_recv()

        forward(q).start()

    pass_on(0)
    make_grad(0, ga)
    pass_on(1)

    for q in range(2):

        @pl.when(c != r)
        def _():
            copy(
                mine_at(q), final_at(x, q), out_send.at[1, q], out_recv.at[1, q], near(2)
            ).wait_recv()

    for q in range(2):
        copy(
            relay_at(q), final_at(1 - x, q), out_send.at[3, q], out_recv.at[3, q], near(2)
        ).wait_recv()
    gb[...] = final[...]

    for v in range(2):
        for d in range(1, SIDE):
            rs_copy(v, d).wait_send()
            ag_copy(v, d).wait_send()
            sum_copy(v, d).wait_send()
        for one in plane_copies(v):
            one.wait_send()
    b_swap.wait_send()
    swap.wait_send()
    forward(0).wait_send()
    forward(1).wait_send()

    @pl.when(c != r)
    def _():
        for q in range(2):
            copy(
                mine_at(q), relay_at(q), out_send.at[1, q], out_recv.at[1, q], near(2)
            ).wait_send()
        copy(raw_b.at[mine, :], half_b, b_send.at[1], b_recv.at[1], near(2)).wait_send()

    @pl.when(flip != r)
    def _():
        for q in range(2):
            copy(
                half_in_at(q), relay_at(q), out_send.at[2, q], out_recv.at[2, q], near(2)
            ).wait_send()
        copy(half_b, half_in, b_send.at[2], b_recv.at[2], near(2)).wait_send()


def gram_gradients(view_a, view_b):
    rows, width = view_a.shape
    images = SIDE * rows
    half = rows // 2
    whole = pl.BlockSpec(memory_space=pltpu.VMEM)
    out = jax.ShapeDtypeStruct((rows, width), jnp.float32)
    bf16, f32 = jnp.bfloat16, jnp.float32
    dma = pltpu.SemaphoreType.DMA
    grad_a, grad_b = pl.pallas_call(
        functools.partial(gram_kernel, images),
        out_shape=(out, jax.ShapeDtypeStruct((rows, width), jnp.bfloat16)),
        in_specs=[whole] * 2,
        out_specs=(whole, whole),
        scratch_shapes=[
            pltpu.VMEM((images, width), bf16),
            pltpu.VMEM((images, width), bf16),
            pltpu.VMEM((rows, width), bf16),
            pltpu.VMEM((8, width), f32),
            pltpu.VMEM((half, width), bf16),
            pltpu.VMEM((rows, width), f32),
            pltpu.VMEM((2, 2 * rows + half, rows), bf16),
            pltpu.VMEM((2, SIDE - 1, (2 * rows + half) // SIDE, rows), bf16),
            pltpu.VMEM((2, 2 * rows + half, rows), bf16),
            pltpu.VMEM((2, rows, rows), bf16),
            pltpu.VMEM((2, half, rows), bf16),
            pltpu.VMEM((SIDE, rows, rows), bf16),
            pltpu.VMEM((1, width), f32),
            pltpu.VMEM((2, 8, width), f32),
            pltpu.VMEM((2, SIDE - 1, 8, width), f32),
            pltpu.VMEM((rows, width), bf16),
            pltpu.VMEM((half, width), bf16),
            pltpu.VMEM((half, width), bf16),
            pltpu.VMEM((rows, width), bf16),
            dma((2, SIDE - 1)),
            dma((2, SIDE - 1)),
            dma((2, SIDE - 1)),
            dma((2, SIDE - 1)),
            dma((2, 2)),
            dma((2, 2)),
            dma((2, SIDE - 1)),
            dma((2, SIDE - 1)),
            dma((4, 2)),
            dma((4, 2)),
            dma((3,)),
            dma((3,)),
            dma((3,)),
            dma((3,)),
            dma((2, 3)),
            dma((2, 3)),
            dma,
            dma,
        ],
        compiler_params=pltpu.CompilerParams(
            collective_id=1, has_side_effects=True, vmem_limit_bytes=60 * 2**20
        ),
    )(view_a, view_b)
    return (grad_a, grad_b.astype(jnp.float32))


def solution(mesh):
    square = mesh.shape["row"] == SIDE and mesh.shape["col"] == SIDE
    per_device = gram_gradients if square else per_device_corr
    return jax.shard_map(
        per_device,
        mesh=mesh,
        in_specs=(P(("groups", "col"), "row"), P(("groups", "row"), "col")),
        out_specs=(P(("groups", "col"), "row"), P(("groups", "row"), "col")),
        check_vma=False,
    )
```

```python
import functools

import jax
import jax.numpy as jnp
from jax import lax
from jax.experimental import pallas as pl
from jax.experimental.pallas import tpu as pltpu
from jax.sharding import PartitionSpec as P

EPSILON = 1e-05
OFF_WEIGHT = 0.0051


def standardize(full_view):
    values = full_view.astype(jnp.float32)
    images = values.shape[0]
    column_mean = jnp.sum(values, axis=0) / images
    centered = values - column_mean
    variance = jnp.sum(centered * centered, axis=0) / images
    scale = lax.rsqrt(variance + EPSILON)
    unit_full = centered * scale
    return (unit_full, unit_full.astype(jnp.bfloat16), scale)


def per_device_corr(view_a, view_b):
    rows_a, width_a = view_a.shape
    rows_b, width_b = view_b.shape
    col_count = lax.axis_size("col")
    row_index = lax.axis_index("row")
    col_index = lax.axis_index("col")
    full_a = lax.all_gather(view_a, "col", axis=0, tiled=True)
    full_b = lax.all_gather(view_b, "row", axis=0, tiled=True)
    images = full_a.shape[0]
    unit_a, norm_a, scale_a = standardize(full_a)
    unit_b, norm_b, scale_b = standardize(full_b)
    correlation = (
        lax.dot_general(
            norm_a, norm_b, (((0,), (0,)), ((), ())), preferred_element_type=jnp.float32
        )
        / images
    )
    row_ids = row_index * width_a + jnp.arange(width_a)
    col_ids = col_index * width_b + jnp.arange(width_b)
    on_diagonal = row_ids[:, None] == col_ids[None, :]
    grad_corr = jnp.where(
        on_diagonal, 2.0 * (correlation - 1.0), 2.0 * OFF_WEIGHT * correlation
    ).astype(jnp.bfloat16)
    slab = norm_b
    back_a = lax.psum_scatter(
        lax.dot_general(
            slab, grad_corr, (((1,), (1,)), ((), ())), preferred_element_type=jnp.float32
        ),
        "col",
        scatter_dimension=0,
        tiled=True,
    )
    own_a = lax.dynamic_slice_in_dim(unit_a, col_index * rows_a, rows_a, 0)
    sums_a = jnp.stack([jnp.sum(back_a, axis=0), jnp.sum(back_a * own_a, axis=0)])
    slab = norm_a
    back_b = lax.psum_scatter(
        jnp.dot(slab, grad_corr, preferred_element_type=jnp.float32),
        "row",
        scatter_dimension=0,
        tiled=True,
    )
    own_b = lax.dynamic_slice_in_dim(unit_b, row_index * rows_b, rows_b, 0)
    sums_b = jnp.stack([jnp.sum(back_b, axis=0), jnp.sum(back_b * own_b, axis=0)])
    whole_width = width_b * col_count
    placed_b = lax.dynamic_update_slice(
        jnp.zeros((2, whole_width), jnp.float32), sums_b, (0, col_index * width_b)
    )
    placed_a = lax.dynamic_update_slice(
        jnp.zeros((2, whole_width), jnp.float32), sums_a, (0, row_index * width_a)
    )
    stacked = jnp.concatenate([placed_a, placed_b], axis=0)
    totals = lax.psum(stacked, ("row", "col"))
    total_b = lax.dynamic_slice_in_dim(totals[-2:], col_index * width_b, width_b, 1)
    total_a = lax.dynamic_slice_in_dim(totals[0:2], row_index * width_a, width_a, 1)
    grad_a = scale_a * (back_a - total_a[0] / images - own_a * (total_a[1] / images))
    grad_b = scale_b * (back_b - total_b[0] / images - own_b * (total_b[1] / images))
    return (grad_a, grad_b)


MESH = pl.DeviceIdType.MESH
SIDE = 4
TILE = 256


def gram_kernel(
    images,
    xa,
    raw_b,
    ga,
    gb,
    na,
    nb,
    xb,
    stats,
    half_b,
    back_b,
    part,
    landed,
    gram,
    next_row,
    cross,
    band,
    direct,
    sums,
    sums_in,
    grad_send,
    half_in,
    relay,
    final,
    rs_send,
    rs_recv,
    ag_send,
    ag_recv,
    plane_send,
    plane_recv,
    sum_send,
    sum_recv,
    out_send,
    out_recv,
    a_send,
    a_recv,
    b_send,
    b_recv,
    bg_send,
    bg_recv,
    local_sem,
    own_sem,
):
    g = lax.axis_index("groups")
    r = lax.axis_index("row")
    c = lax.axis_index("col")
    rows, width = xa.shape
    half = rows // 2
    chunk = part.shape[1] // SIDE
    x = c // 2
    lo = c % 2
    flip = (c + 2) % SIDE
    meet = 2 * x + r % 2
    weight = 2.0 * OFF_WEIGHT
    own = pl.ds(pl.multiple_of(c * rows, rows), rows)
    mine = pl.ds(pl.multiple_of(x * half, half), half)
    theirs = pl.ds(pl.multiple_of((1 - x) * half, half), half)
    straight = r // 2 == x
    sibling = (g, r, c + 1 - 2 * lo)
    norms, raws, backs = (na, nb), (xa, xb), (ga, back_b)

    def near(d):
        return (g, r, (c + d) % SIDE)

    def far(d):
        return (g, (r + d) % SIDE, c)

    def copy(src, dst, send, recv, to):
        return pltpu.make_async_remote_copy(
            src_ref=src,
            dst_ref=dst,
            send_sem=send,
            recv_sem=recv,
            device_id=to,
            device_id_type=MESH,
        )

    barrier = pltpu.get_barrier_semaphore()
    for d in range(1, SIDE):
        pl.semaphore_signal(barrier, inc=1, device_id=near(d), device_id_type=MESH)
        pl.semaphore_signal(barrier, inc=1, device_id=far(d), device_id_type=MESH)
    odd = (r + c) % 2 == 1

    @pl.when(odd)
    def _():
        for plane in (c, flip):
            pl.semaphore_signal(
                barrier, inc=1, device_id=(g, plane, meet), device_id_type=MESH
            )
        pl.semaphore_wait(barrier, 2 * SIDE)

    @pl.when(jnp.logical_not(odd))
    def _():
        pl.semaphore_wait(barrier, 2 * (SIDE - 1))

    def chunk_at(owner):
        return pl.ds(pl.multiple_of(owner * chunk, 16), chunk)

    def make_part(v):
        norm = norms[v]

        def body(i, carry):
            left = jnp.where(i < 4, c * rows + (i % 2) * half, lo * rows + x * half)
            right = jnp.where(i < 2, c, jnp.where(i < 4, (c + 1) % SIDE, lo + 2)) * rows
            a = norm[pl.ds(pl.multiple_of(left, half), half), :]
            b = norm[pl.ds(pl.multiple_of(right, rows), rows), :]
            t = lax.dot_general(
                a, b, (((1,), (1,)), ((), ())), preferred_element_type=jnp.float32
            )
            part[v, pl.ds(pl.multiple_of(i * half, half), half), :] = t.astype(jnp.bfloat16)
            return carry

        lax.fori_loop(0, 5, body, 0)

    def rs_copy(v, d):
        owner = (r + d) % SIDE
        return copy(
            part.at[v, chunk_at(owner), :],
            landed.at[v, d - 1],
            rs_send.at[v, d - 1],
            rs_recv.at[v, d - 1],
            far(d),
        )

    def ag_copy(v, d):
        return copy(
            gram.at[v, chunk_at(r), :],
            gram.at[v, chunk_at(r), :],
            ag_send.at[v, d - 1],
            ag_recv.at[v, d - 1],
            far(d),
        )

    def ag_arrival(v, d):
        owner = (r + SIDE - d) % SIDE
        return copy(
            gram.at[v, chunk_at(owner), :],
            gram.at[v, chunk_at(owner), :],
            ag_send.at[v, d - 1],
            ag_recv.at[v, d - 1],
            far(d),
        )

    def reduce(v):
        for d in range(1, SIDE):
            rs_copy(v, d).wait_recv()
        total = part[v, chunk_at(r), :].astype(jnp.float32)
        for d in range(1, SIDE):
            total = total + landed[v, d - 1].astype(jnp.float32)
        gram[v, chunk_at(r), :] = total.astype(jnp.bfloat16)
        for d in range(1, SIDE):
            ag_copy(v, d).start()

    def plane_copies(v):
        return (
            copy(
                gram.at[v, pl.ds(rows, rows), :],
                next_row.at[v],
                plane_send.at[v, 0],
                plane_recv.at[v, 0],
                near(1),
            ),
            copy(
                gram.at[v, pl.ds(2 * rows, half), :],
                cross.at[v],
                plane_send.at[v, 1],
                plane_recv.at[v, 1],
                near(2),
            ),
        )

    def share(v):
        for d in range(1, SIDE):
            ag_arrival(v, d).wait_recv()
        for one in plane_copies(v):
            one.start()

    def turned(block):
        return block.astype(jnp.float32).T.astype(jnp.bfloat16)

    def make_band(v):
        for one in plane_copies(v):
            one.wait_recv()
        band[c] = gram[v, pl.ds(0, rows), :]
        band[(c + 1) % SIDE] = gram[v, pl.ds(rows, rows), :]
        band[(c + 3) % SIDE] = turned(next_row[v])

        @pl.when(x == 0)
        def _():
            band[flip, pl.ds(0, half), :] = gram[v, pl.ds(2 * rows, half), :]
            band[flip, pl.ds(half, half), :] = cross[v]

        @pl.when(x == 1)
        def _():
            band[flip, :, pl.ds(0, half)] = turned(cross[v])
            band[flip, :, pl.ds(half, half)] = turned(gram[v, pl.ds(2 * rows, half), :])

    def unit_of(w, columns):
        mean = stats[pl.ds(2 * w, 1), columns]
        scale = stats[pl.ds(2 * w + 1, 1), columns]
        return (raws[w][:, columns].astype(jnp.float32) - mean) * scale, scale

    def sum_copy(w, d):
        return copy(
            sums.at[w],
            sums_in.at[w, d - 1],
            sum_send.at[w, d - 1],
            sum_recv.at[w, d - 1],
            near(d),
        )

    def make_back(w):
        norm, other, back_ref = norms[w], norms[1 - w], backs[w]

        def body(j, carry):
            columns = pl.ds(pl.multiple_of(j * TILE, TILE), TILE)
            mixed = jnp.zeros((rows, TILE), jnp.float32)
            for block in range(SIDE):
                mixed = mixed + jnp.dot(
                    band[block],
                    norm[pl.ds(block * rows, rows), columns],
                    preferred_element_type=jnp.float32,
                )
            term = direct[:, columns] * other[own, columns].astype(jnp.float32)
            back = (weight / images) * mixed + term
            unit, _ = unit_of(w, columns)
            back_ref[:, columns] = back
            sums[w, pl.ds(0, 1), columns] = jnp.sum(back, axis=0, keepdims=True)
            sums[w, pl.ds(1, 1), columns] = jnp.sum(back * unit, axis=0, keepdims=True)
            return carry

        lax.fori_loop(0, width // TILE, body, 0)
        for d in range(1, SIDE):
            sum_copy(w, d).start()

    def make_grad(w, target):
        for d in range(1, SIDE):
            sum_copy(w, d).wait_recv()

        def body(j, carry):
            columns = pl.ds(pl.multiple_of(j * TILE, TILE), TILE)
            total = sums[w, pl.ds(0, 2), columns]
            for d in range(1, SIDE):
                total = total + sums_in[w, d - 1, pl.ds(0, 2), columns]
            total = total / images
            unit, scale = unit_of(w, columns)
            grad = scale * (backs[w][:, columns] - total[0:1] - unit * total[1:2])
            target[:, columns] = grad.astype(target.dtype)
            return carry

        lax.fori_loop(0, width // TILE, body, 0)

    def make_direct():
        def body(i, acc):
            lines = pl.ds(pl.multiple_of(i * 16, 16), 16)
            prod = na[lines, :].astype(jnp.float32) * nb[lines, :].astype(jnp.float32)
            return acc + prod[0:8] + prod[8:16]

        acc = lax.fori_loop(0, images // 16, body, jnp.zeros((8, width), jnp.float32))
        diagonal = jnp.sum(acc, axis=0, keepdims=True) / images
        rounded = (2.0 * (diagonal - 1.0)).astype(jnp.bfloat16).astype(jnp.float32)
        direct[...] = rounded - weight * diagonal

    def block_of(b):
        return pl.ds(pl.multiple_of(b * rows, rows), rows)

    def half_of(b, h):
        return pl.ds(pl.multiple_of(b * rows + h * half, half), half)

    def lines_of(i):
        return pl.ds(pl.multiple_of(i * 32, 32), 32)

    def fold(values):
        return values[0:8] + values[8:16] + values[16:24] + values[24:32]

    def standardize_in_place(w):
        norm = norms[w]
        zero = jnp.zeros((8, width), jnp.float32)

        def add(i, acc):
            return acc + fold(norm[lines_of(i), :].astype(jnp.float32))

        acc = lax.fori_loop(0, images // 32, add, zero)
        mean = jnp.sum(acc, axis=0, keepdims=True) / images
        stats[pl.ds(2 * w, 1), :] = mean

        def add_square(i, acc):
            centered = norm[lines_of(i), :].astype(jnp.float32) - stats[pl.ds(2 * w, 1), :]
            return acc + fold(centered * centered)

        acc = lax.fori_loop(0, images // 32, add_square, zero)
        variance = jnp.sum(acc, axis=0, keepdims=True) / images
        stats[pl.ds(2 * w + 1, 1), :] = lax.rsqrt(variance + EPSILON)

        def write(i, carry):
            centered = norm[lines_of(i), :].astype(jnp.float32) - stats[pl.ds(2 * w, 1), :]
            unit = centered * stats[pl.ds(2 * w + 1, 1), :]
            norm[lines_of(i), :] = unit.astype(jnp.bfloat16)
            return carry

        lax.fori_loop(0, images // 32, write, 0)

    sums[...] = jnp.zeros_like(sums)

    a_side = copy(xa, na.at[own, :], a_send.at[0], a_recv.at[0], sibling)
    a_cross = copy(xa, na.at[own, :], a_send.at[1], a_recv.at[1], near(2))
    a_pass = copy(
        na.at[block_of(flip), :],
        na.at[block_of(flip), :],
        a_send.at[2],
        a_recv.at[2],
        sibling,
    )
    a_own = pltpu.make_async_copy(xa, na.at[own, :], own_sem)
    b_swap = copy(raw_b.at[theirs, :], half_b, b_send.at[0], b_recv.at[0], near(2))
    b_place = nb.at[half_of(r, x), :]

    def b_hop(src, plane, send):
        @pl.when(straight)
        def _():
            copy(
                src, b_place, b_send.at[send], b_recv.at[1], (g, plane, meet)
            ).start()

        @pl.when(jnp.logical_not(straight))
        def _():
            copy(
                src, b_place, b_send.at[send], b_recv.at[2], (g, plane, meet)
            ).start()

    a_cross.start()
    a_side.start()
    a_own.start()

    @pl.when(c != r)
    def _():
        b_hop(raw_b.at[mine, :], c, 1)

    @pl.when(c == r)
    def _():
        stay = pltpu.make_async_copy(raw_b.at[mine, :], b_place, local_sem)
        stay.start()
        stay.wait()

    a_cross.wait_recv()
    b_swap.start()
    a_pass.start()

    def b_spread(k):
        block = c if k == 0 else flip
        here = nb.at[half_of(block, x), :]
        came = nb.at[half_of(flip if k == 0 else c, 1 - x), :]
        return (
            copy(here, here, bg_send.at[k, 0], bg_recv.at[k, 0], sibling),
            copy(here, here, bg_send.at[k, 1], bg_recv.at[k, 1], near(2)),
            copy(came, came, bg_send.at[k, 2], bg_recv.at[k, 2], sibling),
        )

    other_col = c + 1 - 2 * lo
    far_col = (other_col + 2) % SIDE

    def arrived(ref, place, recv):
        copy(ref.at[place, :], ref.at[place, :], a_send.at[0], recv, near(2)).wait_recv()

    a_own.wait()
    arrived(na, block_of(other_col), a_recv.at[0])
    arrived(na, block_of(far_col), a_recv.at[2])
    a_side.wait_send()
    a_cross.wait_send()
    a_pass.wait_send()
    standardize_in_place(0)
    make_part(0)
    for d in range(1, SIDE):
        rs_copy(0, d).start()
    b_swap.wait_recv()

    @pl.when(flip != r)
    def _():
        b_hop(half_b, flip, 2)

    @pl.when(flip == r)
    def _():
        stay = pltpu.make_async_copy(half_b, b_place, local_sem)
        stay.start()
        stay.wait()

    @pl.when(c != r)
    def _():
        here = nb.at[half_of(c, x), :]
        copy(here, here, b_send.at[1], b_recv.at[1], near(2)).wait_recv()

    b_spread(0)[1].start()
    b_spread(0)[0].start()

    @pl.when(flip != r)
    def _():
        here = nb.at[half_of(flip, x), :]
        copy(here, here, b_send.at[2], b_recv.at[2], near(2)).wait_recv()

    b_spread(1)[1].start()
    b_spread(1)[0].start()

    reduce(0)

    for k in range(2):
        arrived(nb, half_of(flip if k == 0 else c, 1 - x), bg_recv.at[k, 1])
        b_spread(k)[2].start()
    for k in range(2):
        arrived(nb, half_of(other_col if k == 0 else far_col, x), bg_recv.at[k, 0])
        arrived(nb, half_of(far_col if k == 0 else other_col, 1 - x), bg_recv.at[k, 2])
    for k in range(2):
        for one in b_spread(k):
            one.wait_send()
    keep = pltpu.make_async_copy(nb.at[own, :], xb, local_sem)
    keep.start()
    keep.wait()
    standardize_in_place(1)
    make_part(1)
    for d in range(1, SIDE):
        rs_copy(1, d).start()
    make_direct()
    share(0)
    make_band(0)
    make_back(1)
    reduce(1)
    make_grad(1, grad_send)

    quarter = half // 2

    def final_at(h, q):
        return final.at[
            pl.ds(pl.multiple_of(h * half + q * quarter, quarter), quarter), :
        ]

    def mine_at(q):
        return grad_send.at[
            pl.ds(pl.multiple_of(x * half + q * quarter, quarter), quarter), :
        ]

    def relay_at(q):
        return relay.at[pl.ds(q * quarter, quarter), :]

    def half_in_at(q):
        return half_in.at[pl.ds(q * quarter, quarter), :]

    swap = copy(
        grad_send.at[theirs, :], half_in, out_send.at[0, 0], out_recv.at[0, 0], near(2)
    )
    swap.start()

    def hop(src, plane, send):
        to = (g, plane, meet)
        for q in range(2):
            piece = src(q)

            @pl.when(straight)
            def _():
                copy(
                    piece, final_at(x, q), out_send.at[send, q], out_recv.at[1, q], to
                ).start()

            @pl.when(jnp.logical_not(straight))
            def _():
                copy(
                    piece, relay_at(q), out_send.at[send, q], out_recv.at[2, q], to
                ).start()

    @pl.when(c != r)
    def _():
        hop(mine_at, c, 1)

    @pl.when(c == r)
    def _():
        stay = pltpu.make_async_copy(grad_send.at[mine, :], final.at[mine, :], local_sem)
        stay.start()
        stay.wait()

    swap.wait_recv()

    @pl.when(flip != r)
    def _():
        hop(half_in_at, flip, 2)

    @pl.when(flip == r)
    def _():
        stay = pltpu.make_async_copy(half_in, relay, local_sem)
        stay.start()
        stay.wait()

    share(1)
    make_band(1)
    make_back(0)

    def forward(q):
        return copy(
            relay_at(q), final_at(x, q), out_send.at[3, q], out_recv.at[3, q], near(2)
        )

    def pass_on(q):
        @pl.when(flip != r)
        def _():
            copy(
                relay_at(q), relay_at(q), out_send.at[2, q], out_recv.at[2, q], near(2)
            ).wait_recv()

        forward(q).start()

    pass_on(0)
    make_grad(0, ga)
    pass_on(1)

    for q in range(2):

        @pl.when(c != r)
        def _():
            copy(
                mine_at(q), final_at(x, q), out_send.at[1, q], out_recv.at[1, q], near(2)
            ).wait_recv()

    for q in range(2):
        copy(
            relay_at(q), final_at(1 - x, q), out_send.at[3, q], out_recv.at[3, q], near(2)
        ).wait_recv()
    gb[...] = final[...]

    for v in range(2):
        for d in range(1, SIDE):
            rs_copy(v, d).wait_send()
            ag_copy(v, d).wait_send()
            sum_copy(v, d).wait_send()
        for one in plane_copies(v):
            one.wait_send()
    b_swap.wait_send()
    swap.wait_send()
    forward(0).wait_send()
    forward(1).wait_send()

    @pl.when(c != r)
    def _():
        for q in range(2):
            copy(
                mine_at(q), relay_at(q), out_send.at[1, q], out_recv.at[1, q], near(2)
            ).wait_send()
        copy(raw_b.at[mine, :], half_b, b_send.at[1], b_recv.at[1], near(2)).wait_send()

    @pl.when(flip != r)
    def _():
        for q in range(2):
            copy(
                half_in_at(q), relay_at(q), out_send.at[2, q], out_recv.at[2, q], near(2)
            ).wait_send()
        copy(half_b, half_in, b_send.at[2], b_recv.at[2], near(2)).wait_send()


def gram_gradients(view_a, view_b):
    rows, width = view_a.shape
    images = SIDE * rows
    half = rows // 2
    whole = pl.BlockSpec(memory_space=pltpu.VMEM)
    out = jax.ShapeDtypeStruct((rows, width), jnp.float32)
    bf16, f32 = jnp.bfloat16, jnp.float32
    dma = pltpu.SemaphoreType.DMA
    grad_a, grad_b = pl.pallas_call(
        functools.partial(gram_kernel, images),
        out_shape=(out, jax.ShapeDtypeStruct((rows, width), jnp.bfloat16)),
        in_specs=[whole] * 2,
        out_specs=(whole, whole),
        scratch_shapes=[
            pltpu.VMEM((images, width), bf16),
            pltpu.VMEM((images, width), bf16),
            pltpu.VMEM((rows, width), bf16),
            pltpu.VMEM((8, width), f32),
            pltpu.VMEM((half, width), bf16),
            pltpu.VMEM((rows, width), f32),
            pltpu.VMEM((2, 2 * rows + half, rows), bf16),
            pltpu.VMEM((2, SIDE - 1, (2 * rows + half) // SIDE, rows), bf16),
            pltpu.VMEM((2, 2 * rows + half, rows), bf16),
            pltpu.VMEM((2, rows, rows), bf16),
            pltpu.VMEM((2, half, rows), bf16),
            pltpu.VMEM((SIDE, rows, rows), bf16),
            pltpu.VMEM((1, width), f32),
            pltpu.VMEM((2, 8, width), f32),
            pltpu.VMEM((2, SIDE - 1, 8, width), f32),
            pltpu.VMEM((rows, width), bf16),
            pltpu.VMEM((half, width), bf16),
            pltpu.VMEM((half, width), bf16),
            pltpu.VMEM((rows, width), bf16),
            dma((2, SIDE - 1)),
            dma((2, SIDE - 1)),
            dma((2, SIDE - 1)),
            dma((2, SIDE - 1)),
            dma((2, 2)),
            dma((2, 2)),
            dma((2, SIDE - 1)),
            dma((2, SIDE - 1)),
            dma((4, 2)),
            dma((4, 2)),
            dma((3,)),
            dma((3,)),
            dma((3,)),
            dma((3,)),
            dma((2, 3)),
            dma((2, 3)),
            dma,
            dma,
        ],
        compiler_params=pltpu.CompilerParams(
            collective_id=1, has_side_effects=True, vmem_limit_bytes=60 * 2**20
        ),
    )(view_a, view_b)
    return (grad_a, grad_b.astype(jnp.float32))


def solution(mesh):
    square = mesh.shape["row"] == SIDE and mesh.shape["col"] == SIDE
    per_device = gram_gradients if square else per_device_corr
    return jax.shard_map(
        per_device,
        mesh=mesh,
        in_specs=(P(("groups", "col"), "row"), P(("groups", "row"), "col")),
        out_specs=(P(("groups", "col"), "row"), P(("groups", "row"), "col")),
        check_vma=False,
    )
```
